256 devices in a mesh: fsdp: 32 (over x, y, z_lo), tensor: 8 (over z_hi, core).
Axes of the slice: x: 4, y: 4, z: 8 (z_hi: 4, z_lo: 2; z = z_hi * 2 + z_lo), core: 2. Of those that a mesh axis runs over, the one named last changes fastest.
Arguments:
- activations: bfloat16 [2, 20480, 27648], P(None, 'fsdp', 'tensor'), may hold values from -6 to 6
- out_grads: bfloat16 [2, 20480, 5120], P(None, 'fsdp', 'tensor'), may hold values from -6 to 6
- in_maps: bfloat16 [2, 256, 27648], P(None, 'fsdp', 'tensor'), may hold values from -0.0390625 to 0.0390625
- out_maps: bfloat16 [2, 256, 5120], P(None, 'fsdp', 'tensor'), may hold values from -0.078125 to 0.078125
- col_scale: float32 [2, 27648], P(None, 'tensor'), may hold values from 0.3 to 3
- row_scale: float32 [2, 5120], P(None, 'tensor'), may hold values from 0.3 to 3
- white_left: float32 [2, 256, 256], replicated, may hold values from -0.375 to 0.375
- white_right: float32 [2, 256, 256], replicated, may hold values from -0.375 to 0.375
- doc_lengths: int32 [32, 4], P('fsdp'), may hold values from 1 to 320, 640 in all within a row
- queries: bfloat16 [512, 2, 256, 256], P('fsdp', None, None, 'tensor'), may hold values from -6 to 6
Outputs:
- scores: float32 [128, 512], P('fsdp', 'tensor')
The draws below stay inside these ranges and needn't reach their ends.
Inputs may be any that keep to these rules, and one draw needn't show every extreme that they name: `doc_lengths`: each row sums to 640; each row's largest count is exactly 320.
All inputs are finite; a program needn't handle non-finite values.
Results may differ from the reference program's by a relative error of at most 0.007.
Values may be sent and summed in bfloat16 or wider, within the bound.
No kernel may reach another device: no remote copies, remote signals or barrier semaphores. Data moves between devices by JAX's collectives and lax.ppermute only.
A program may use at most 128 MiB of HBM per device.

```python
import math
import jax
import jax.numpy as jnp
import numpy as np
from jax import lax

D = 5120
FF = 27648
KOUT = 256
KIN = 256
LAYERS = 2
TOK_DEV = 640
DOC_DEV = 4
OWNERS = 32
TOKENS = 20480
DOCS = 128
QUERIES = 512
FEAT = 131072


def steps_of(key, shape, pieces, smallest, top_value):
    factor_of, own = 1.0, jax.random.fold_in(key, 6)
    for dim, shards_of in pieces:
        steps = jnp.exp(jax.random.uniform(jax.random.fold_in(own, dim), (shards_of,), jnp.float32, smallest / len(pieces), top_value / len(pieces)))
        factor_of = factor_of * jnp.repeat(steps, shape[dim] // shards_of).reshape([-1 if axis == dim else 1 for axis in range(len(shape))])
    return factor_of


def profile(count, total, most, slope):
    loads = [(1 << 20) // math.isqrt(rank ** slope) + 1 for rank in range(2, count + 1)]
    spare, holding = total - most - (count - 1), [1] * (count - 1)
    while spare > 0:
        candidates = [i for i in range(count - 1) if holding[i] < most]
        whole, left = sum([loads[i] for i in candidates]), spare
        for i in candidates:
            more = min(most - holding[i], max(1, left * loads[i] // whole), spare)
            holding[i] = holding[i] + more
            spare = spare - more
    return np.array([most] + holding)


def ragged(stream_key, count, total, reach, slope):
    if count == 2:
        one = jax.random.randint(stream_key, (), max(1, total - reach), min(reach, total - 1) + 1)
        return jnp.stack([one, total - one])
    sizes = jnp.asarray(profile(count, total, reach, slope), jnp.int32)
    couples = (count - 1) // 2
    giver, sink = sizes[1:1 + 2 * couples:2], sizes[2:2 + 2 * couples:2]
    slack = jnp.minimum(giver - 1, reach - sink)
    moved = jax.random.randint(jax.random.fold_in(stream_key, 1), (couples,), 0, 1 << 20) % (slack + 1)
    sizes = sizes.at[1:1 + 2 * couples:2].set(giver - moved).at[2:2 + 2 * couples:2].set(sink + moved)
    return sizes[jax.random.permutation(jax.random.fold_in(stream_key, 2), count)]


def noise(stream_key, shape, spread, limit, shards=(), kind=jnp.bfloat16):
    loudness = steps_of(stream_key, shape, shards, -0.22, 0.18) if shards else 1.0
    result = jax.random.normal(stream_key, shape, jnp.float32) * spread * loudness
    return jnp.minimum(jnp.maximum(result, -limit), limit).astype(kind)


def setup_inputs(seed: int = 0) -> dict:
    seeds = jax.random.split(jax.random.key(seed), 11)
    return {
        "activations": noise(seeds[0], (LAYERS, TOKENS, FF), 1.0, 6.0, ((1, 32), (2, 8))),
        "out_grads": noise(seeds[1], (LAYERS, TOKENS, D), 1.0, 6.0, ((1, 32), (2, 8))),
        "in_maps": noise(seeds[2], (LAYERS, KIN, FF), FF ** -0.5, 0.0390625, ((1, 32), (2, 8))),
        "out_maps": noise(seeds[3], (LAYERS, KOUT, D), D ** -0.5, 0.078125, ((1, 32), (2, 8))),
        "col_scale": jnp.clip(jnp.exp(math.log(3.0) - 2.3025851 * jax.random.uniform(seeds[4], (LAYERS, FF), jnp.float32) ** steps_of(seeds[4], (LAYERS, FF), ((1, 8),), -0.2, 0.2)), 0.3, 3.0),
        "row_scale": jnp.clip(jnp.exp(math.log(3.0) - 2.3025851 * jax.random.uniform(seeds[5], (LAYERS, D), jnp.float32) ** steps_of(seeds[5], (LAYERS, D), ((1, 8),), -0.2, 0.2)), 0.3, 3.0),
        "white_left": noise(seeds[6], (LAYERS, KOUT, KOUT), KOUT ** -0.5, 0.375, (), jnp.float32),
        "white_right": noise(seeds[7], (LAYERS, KIN, KIN), KIN ** -0.5, 0.375, (), jnp.float32),
        "doc_lengths": jax.vmap(lambda own: ragged(own, DOC_DEV, TOK_DEV, TOK_DEV // 2, 2))(jax.random.split(seeds[8], OWNERS)).reshape((OWNERS, DOC_DEV)).astype(jnp.int32),
        "queries": noise(seeds[9], (QUERIES, LAYERS, KOUT, KIN), 1.0, 6.0, ((0, 32), (3, 8))),
    }


def layer_features(member, left_layer, right_layer):
    masked = member.T[:, :, None] * left_layer[None]
    count = masked.shape[0]
    width = masked.shape[2]
    stacked = masked.transpose(0, 2, 1).reshape(count * width, masked.shape[1])
    product = jnp.dot(stacked, right_layer, preferred_element_type=jnp.float32)
    return product.reshape(count, width, right_layer.shape[1])

def owner_features(inputs):
    lengths, left_own, right_own = inputs
    ends = jnp.cumsum(lengths)
    starts = ends - lengths
    places = jnp.arange(left_own.shape[1], dtype=jnp.int32)[:, None]
    member = ((places >= starts[None, :]) & (places < ends[None, :])).astype(jnp.bfloat16)
    features = jnp.stack([layer_features(member, left_own[layer], right_own[layer]) for layer in range(left_own.shape[0])], axis=1)
    meansq = lax.optimization_barrier(jnp.mean(features * features, axis=(1, 2, 3)))
    scaled = features * lax.rsqrt(meansq + 1e-06)[:, None, None, None]
    return scaled.astype(jnp.bfloat16).reshape(features.shape[0], -1)

def reference(activations, out_grads, in_maps, out_maps, col_scale, row_scale, white_left, white_right, doc_lengths, queries):
    scaled_in = (in_maps.astype(jnp.float32) * col_scale[:, None, :]).astype(jnp.bfloat16)
    scaled_out = (out_maps.astype(jnp.float32) * row_scale[:, None, :]).astype(jnp.bfloat16)
    lefts = []
    rights = []
    for layer in range(LAYERS):
        proj_in = jnp.dot(activations[layer], scaled_in[layer].T, preferred_element_type=jnp.float32)
        proj_out = jnp.dot(out_grads[layer], scaled_out[layer].T, preferred_element_type=jnp.float32)
        rights.append(jnp.dot(proj_in, white_right[layer], precision=lax.Precision.HIGHEST).astype(jnp.bfloat16))
        lefts.append(jnp.dot(proj_out, white_left[layer].T, precision=lax.Precision.HIGHEST).astype(jnp.bfloat16))
    left_all = jnp.stack(lefts).reshape(LAYERS, OWNERS, TOK_DEV, KOUT).transpose(1, 0, 2, 3)
    right_all = jnp.stack(rights).reshape(LAYERS, OWNERS, TOK_DEV, KIN).transpose(1, 0, 2, 3)
    doc_unit = lax.map(owner_features, (doc_lengths, left_all, right_all)).reshape(DOCS, FEAT)
    query_f = queries.astype(jnp.float32)
    query_ms = lax.optimization_barrier(jnp.mean(query_f * query_f, axis=(1, 2, 3)))
    query_unit = (query_f * lax.rsqrt(query_ms + 1e-06)[:, None, None, None]).astype(jnp.bfloat16).reshape(QUERIES, FEAT)
    total = jnp.dot(doc_unit, query_unit.T, preferred_element_type=jnp.float32)
    return total * (1.0 / math.sqrt(FEAT))
```

```python
import math

import jax
import jax.numpy as jnp
from jax import lax
from jax.sharding import PartitionSpec as P

F32, BF16 = jnp.float32, jnp.bfloat16
NT = (((1,), (1,)), ((), ()))


def core_swap(value):
    pairs = [(place, place ^ 1) for place in range(lax.axis_size("tensor"))]
    return lax.ppermute(value, "tensor", pairs)


def chip_shift(value, step):
    size = lax.axis_size("tensor")
    return lax.ppermute(value, "tensor", [(src, (src + 2 * step) % size) for src in range(size)])


def relative_rows(weight, core, chip):
    rows, depth = weight.shape
    parts = weight.reshape(2, 4, rows // 8, depth)
    parts = jnp.where(core == 0, parts, parts[::-1])
    doubled = jnp.concatenate([parts, parts], axis=1)
    parts = lax.dynamic_slice_in_dim(doubled, chip, 4, axis=1)
    return parts.reshape(rows, depth)


def absolute_chunks(parts, core, chip):
    two = jnp.roll(parts, 2, axis=2)
    parts = jnp.where(chip >= 2, two, parts)
    one = jnp.roll(parts, 1, axis=2)
    parts = jnp.where(chip % 2 == 1, one, parts)
    return jnp.where(core == 0, parts, parts[:, ::-1])


def tensor_sum(total):
    other = core_swap(total[:, 1].astype(BF16))
    both = total[:, 0] + other.astype(F32)
    sends = [chip_shift(both[:, step].astype(BF16), step) for step in (1, 2, 3)]
    return both[:, 0] + sends[0].astype(F32) + sends[1].astype(F32) + sends[2].astype(F32)


def body(
    activations,
    out_grads,
    in_maps,
    out_maps,
    col_scale,
    row_scale,
    white_left,
    white_right,
    doc_lengths,
    queries,
):
    layers, tokens, hidden = activations.shape
    width = out_grads.shape[2]
    owners = lax.axis_size("fsdp")
    group = lax.axis_size("tensor")
    place = lax.axis_index("tensor")
    chip, core = place // 2, place % 2
    docs = doc_lengths.shape[1]
    own_queries, _, kout, kslice = queries.shape
    kin = kslice * group
    total_queries = own_queries * owners
    count = layers * kout * kin
    pair = layers * kslice // owners

    scaled_in = (in_maps.astype(F32) * col_scale[:, None, :]).astype(BF16)
    scaled_out = (out_maps.astype(F32) * row_scale[:, None, :]).astype(BF16)
    maps = jnp.concatenate([scaled_in, scaled_out], axis=2)
    rows = maps.shape[1]
    maps = maps.reshape(layers * rows, hidden + width)
    query_f = queries.astype(F32)
    query_sq = jnp.sum(query_f * query_f, axis=(1, 2, 3))
    query_hi = lax.reduce_precision(query_sq, 8, 7)
    query_lo = query_sq - query_hi
    squares = jnp.stack([query_hi, query_lo], axis=1).astype(BF16)
    squares = jnp.pad(squares, ((0, 0), (0, 126)))
    slices = queries.transpose(0, 1, 3, 2).reshape(own_queries, owners, pair * kout)
    slices = slices.transpose(1, 0, 2)
    shared = jnp.concatenate([maps, squares], axis=1)
    shared = jnp.broadcast_to(shared[None], (owners,) + shared.shape)
    sent = jnp.concatenate([shared, slices], axis=2)
    got = lax.all_to_all(sent, "fsdp", 0, 0, tiled=True)
    base = hidden + width
    square_got = got[:, :, base : base + 2].astype(F32)
    square_got = (square_got[:, :, 0] + square_got[:, :, 1]).reshape(total_queries)
    query_got = got[:, :, base + 128 :].reshape(total_queries, pair * kout)

    rights, lefts = [], []
    for layer in range(layers):
        block = got[:, layer * rows : (layer + 1) * rows]
        full_in = block[:, :, :hidden].reshape(owners * rows, hidden)
        full_out = block[:, :, hidden:base].reshape(owners * rows, width)
        proj_in = lax.dot_general(full_in, activations[layer], NT, preferred_element_type=F32)
        proj_out = lax.dot_general(full_out, out_grads[layer], NT, preferred_element_type=F32)
        turn = white_right[layer].T.reshape(4, 2, kin // 8, kin).transpose(1, 0, 2, 3)
        turn = relative_rows(turn.reshape(kin, kin), core, chip)
        lean = relative_rows(white_left[layer], core, chip)
        rights.append(jnp.dot(turn, proj_in, precision=lax.Precision.HIGHEST))
        lefts.append(jnp.dot(lean, proj_out, precision=lax.Precision.HIGHEST))
    left = tensor_sum(jnp.stack(lefts).reshape(layers, 2, 4, kout // 8, tokens)).astype(BF16)
    right = tensor_sum(jnp.stack(rights).reshape(layers, 2, 4, kslice, tokens)).astype(BF16)
    around = [left] + [chip_shift(left, -step) for step in (1, 2, 3)]
    around = jnp.stack(around, axis=1)
    around = jnp.stack([around, core_swap(around)], axis=1)
    left_all = absolute_chunks(around, core, chip).reshape(layers, kout, tokens)

    lengths = doc_lengths[0]
    ends = jnp.cumsum(lengths)
    starts = ends - lengths
    spots = jnp.arange(tokens, dtype=jnp.int32)[None, :]
    member = ((spots >= starts[:, None]) & (spots < ends[:, None])).astype(BF16)
    features = []
    for layer in range(layers):
        masked = (right[layer][:, None, :] * member[None]).reshape(kslice * docs, tokens)
        features.append(
            lax.dot_general(masked, left_all[layer], NT, preferred_element_type=F32)
        )
    features = jnp.stack(features)
    doc_sq = jnp.sum((features * features).reshape(layers * kslice, docs, kout), axis=(0, 2))
    doc_sent = features.astype(BF16).reshape(owners, pair * docs, kout)
    doc_got = lax.all_to_all(doc_sent, "fsdp", 0, 0, tiled=True)

    doc_rows = doc_got.reshape(owners * pair * docs, kout)
    half = (jnp.arange(owners * pair * docs) // docs) % pair
    wide = jnp.concatenate(
        [jnp.where((half == one)[:, None], doc_rows, 0) for one in range(pair)], axis=1
    )
    product = lax.dot_general(wide, query_got, NT, preferred_element_type=F32)
    score_sent = product.astype(BF16).reshape(owners, pair * docs, total_queries)
    score_got = lax.all_to_all(score_sent, "fsdp", 0, 0, tiled=True)
    scores = jnp.sum(
        score_got.astype(F32).reshape(owners * pair, docs, total_queries), axis=0
    )
    final = total_queries // group
    doc_row = jnp.tile(jnp.pad(doc_sq, (0, final - docs)), group)
    last = jnp.concatenate([scores, square_got[None], doc_row[None]], axis=0)
    last = jnp.pad(last, ((0, 8 - last.shape[0]), (0, 0)))
    last = last.reshape(8, group, final).transpose(1, 0, 2)
    last = jnp.sum(lax.all_to_all(last, "tensor", 0, 0, tiled=True), axis=0)
    factor = 1.0 / math.sqrt(count)
    doc_scale = lax.rsqrt(last[docs + 1, :docs] / count + 1e-06)
    query_scale = lax.rsqrt(last[docs] / count + 1e-06)
    return last[:docs] * doc_scale[:, None] * query_scale[None, :] * factor


def solution(mesh):
    in_specs = (
        P(None, "fsdp", "tensor"),
        P(None, "fsdp", "tensor"),
        P(None, "fsdp", "tensor"),
        P(None, "fsdp", "tensor"),
        P(None, "tensor"),
        P(None, "tensor"),
        P(),
        P(),
        P("fsdp", None),
        P("fsdp", None, None, "tensor"),
    )
    out_specs = P("fsdp", "tensor")
    return jax.shard_map(body, mesh=mesh, in_specs=in_specs, out_specs=out_specs, check_vma=False)
```

```python
import math

import jax
import jax.numpy as jnp
from jax import lax
from jax.sharding import PartitionSpec as P

F32, BF16 = jnp.float32, jnp.bfloat16
NT = (((1,), (1,)), ((), ()))

MASKS = {"z": 1, "y1": 2, "y3": 6, "x1": 8, "x3": 24}
ORDERS = (
    ("x1", "x3", "y1", "y3"),
    ("x3", "x1", "y3", "y1"),
    ("y1", "y3", "x1", "x3"),
    ("y3", "y1", "x3", "x1"),
)

COMMON = ("x3", "x1", "y3", "y1")


def held_masks(order):
    masks = [0]
    for name in ("z",) + order:
        masks = masks + [mask ^ MASKS[name] for mask in masks]
    return masks


def core_swap(value):
    pairs = [(place, place ^ 1) for place in range(lax.axis_size("tensor"))]
    return lax.ppermute(value, "tensor", pairs)


def chip_shift(value, step):
    size = lax.axis_size("tensor")
    return lax.ppermute(value, "tensor", [(src, (src + 2 * step) % size) for src in range(size)])


def owner_swap(value, step):
    mask = MASKS[step]
    pairs = [(place, place ^ mask) for place in range(lax.axis_size("fsdp"))]
    return lax.ppermute(value, "fsdp", pairs)


def after(value, *others):
    return lax.optimization_barrier((value,) + others)[0]


def tree_gather(block):
    tiles = block.shape[1] // 128
    cuts = [128 * ((tiles * part) // 4) for part in range(5)]
    both = jnp.stack([block, owner_swap(block, "z")])
    chunks = [both[:, :, cuts[part] : cuts[part + 1]] for part in range(4)]
    for step in range(4):
        arrived = [owner_swap(chunk, order[step]) for chunk, order in zip(chunks, ORDERS)]
        chunks = [jnp.concatenate([chunk, new]) for chunk, new in zip(chunks, arrived)]
    return [chunk.reshape(-1, chunk.shape[-1]) for chunk in chunks], cuts


def scale_maps(in_maps, out_maps, col_scale, row_scale):
    scaled = [
        (maps[layer].astype(F32) * scale[layer][None, :]).astype(BF16)
        for maps, scale in ((out_maps, row_scale), (in_maps, col_scale))
        for layer in range(maps.shape[0])
    ]
    return jnp.concatenate(scaled, axis=1)


def common_order(chunk, order):
    parts = chunk.reshape(2, 2, 2, 2, 2, 8, chunk.shape[1])
    axes = [3 - order.index(name) for name in COMMON]
    return parts.transpose(axes + [4, 5, 6]).reshape(chunk.shape)


def one_hot(indices, size):
    return (indices[:, None] == jnp.arange(size, dtype=jnp.int32)[None, :]).astype(F32)


def turned_weights(white_left, white_right, owner, chip, core):
    rows = white_left.shape[1]
    line = jnp.arange(rows, dtype=jnp.int32)
    masks = jnp.asarray(held_masks(COMMON[::-1]), jnp.int32)
    contracted = one_hot((owner ^ jnp.repeat(masks, 8)) * 8 + line % 8, rows)
    away, there = core ^ (line // 128), (chip + line // 32) & 3
    exact = lax.Precision.HIGHEST
    left_rows = one_hot(128 * away + 32 * there + line % 32, rows)
    right_rows = one_hot(64 * there + 32 * away + line % 32, rows)
    left, right = [], []
    for layer in range(white_left.shape[0]):
        half = jnp.dot(left_rows, white_left[layer], precision=exact)
        left.append(lax.dot_general(half, contracted, NT, precision=exact))
        half = lax.dot_general(
            right_rows, white_right[layer], (((1,), (1,)), ((), ())), precision=exact
        )
        right.append(lax.dot_general(half, contracted, NT, precision=exact))
    return left, right


def absolute_chunks(parts, core, chip):
    two = jnp.roll(parts, 2, axis=2)
    parts = jnp.where(chip >= 2, two, parts)
    one = jnp.roll(parts, 1, axis=2)
    parts = jnp.where(chip % 2 == 1, one, parts)
    return jnp.where(core == 0, parts, parts[:, ::-1])


def tensor_sum(parts):
    jobs, rows, tokens = parts.shape[0], parts.shape[1] // 2, parts.shape[2]
    mine, theirs = parts[:, :rows], parts[:, rows:].astype(BF16)
    other = core_swap(theirs)
    both = (mine + other.astype(F32)).reshape(jobs, 4, rows // 4, tokens)
    sends = [chip_shift(both[:, step].astype(BF16), step) for step in (2, 1, 3)]
    total = both[:, 0] + sends[0].astype(F32) + sends[1].astype(F32) + sends[2].astype(F32)
    return total.astype(BF16)


def chip_swap(value, mask):
    pairs = [(src, src ^ (2 * mask)) for src in range(lax.axis_size("tensor"))]
    return lax.ppermute(value, "tensor", pairs)


def body(
    activations,
    out_grads,
    in_maps,
    out_maps,
    col_scale,
    row_scale,
    white_left,
    white_right,
    doc_lengths,
    queries,
):
    layers, tokens, hidden = activations.shape
    width = out_grads.shape[2]
    owners = lax.axis_size("fsdp")
    group = lax.axis_size("tensor")
    place = lax.axis_index("tensor")
    owner = lax.axis_index("fsdp")
    chip, core = place // 2, place % 2
    docs = doc_lengths.shape[1]
    own_queries, _, kout, kslice = queries.shape
    kin = kslice * group
    total_queries = own_queries * owners
    count = layers * kout * kin
    pair = layers * kslice // owners

    left_weights, right_weights = turned_weights(white_left, white_right, owner, chip, core)
    slices = queries.transpose(0, 1, 3, 2).reshape(own_queries, owners, pair * kout)
    slices = slices.transpose(1, 0, 2)
    chunks, cuts = tree_gather(scale_maps(in_maps, out_maps, col_scale, row_scale))

    chunks = [common_order(chunk, order) for chunk, order in zip(chunks, ORDERS)]
    parts = []
    for values, low, weights in (
        (out_grads, 0, left_weights),
        (activations, layers * width, right_weights),
    ):
        wide = values.shape[2]
        for layer in range(layers):
            first, total = low + layer * wide, None
            for index in range(4):
                begin, end = max(cuts[index], first), min(cuts[index + 1], first + wide)
                if begin >= end:
                    continue
                block = chunks[index][:, begin - cuts[index] : end - cuts[index]]
                piece = values[layer][:, begin - first : end - first]
                product = lax.dot_general(block, piece, NT, preferred_element_type=F32)
                total = product if total is None else total + product
            parts.append(jnp.dot(weights[layer], total, precision=lax.Precision.HIGH))
    summed = tensor_sum(jnp.stack(parts))
    left, right = summed[:layers], summed[layers:]
    around = [left] + [chip_shift(left, -step) for step in (1, 2, 3)]
    around = jnp.stack(around, axis=1)
    around = jnp.stack([around, core_swap(around)], axis=1)
    left_all = absolute_chunks(around, core, chip).reshape(layers, kout, tokens)

    lengths = doc_lengths[0]
    ends = jnp.cumsum(lengths)
    starts = ends - lengths
    spots = jnp.arange(tokens, dtype=jnp.int32)[None, :]
    member = ((spots >= starts[:, None]) & (spots < ends[:, None])).astype(BF16)
    features = []
    for layer in range(layers):
        masked = (right[layer][:, None, :] * member[None]).reshape(kslice * docs, tokens)
        features.append(
            lax.dot_general(masked, left_all[layer], NT, preferred_element_type=F32)
        )
    features = jnp.stack(features)
    doc_sq = jnp.sum((features * features).reshape(layers * kslice, docs, kout), axis=(0, 2))
    doc_sent = features.astype(BF16).reshape(owners, pair * docs, 2, kout // 2)
    doc_sent = doc_sent.transpose(0, 2, 1, 3).reshape(owners, 2 * pair * docs, kout // 2)
    sent = jnp.concatenate([slices, doc_sent], axis=2)
    got = lax.all_to_all(sent, "fsdp", 0, 0, tiled=True)
    query_got = got[:, :, : pair * kout].reshape(total_queries, pair * kout)
    query_f = query_got.astype(F32)
    query_sq = jnp.sum(query_f * query_f, axis=1)
    query_high = lax.reduce_precision(query_sq, 8, 7)
    query_low = query_sq - query_high

    doc_got = got[:, :, pair * kout :].reshape(owners, 2, pair * docs, kout // 2)
    doc_rows = doc_got.transpose(0, 2, 1, 3).reshape(owners * pair * docs, kout)
    half = (jnp.arange(owners * pair * docs) // docs) % pair
    wide = jnp.concatenate(
        [jnp.where((half == one)[:, None], doc_rows, 0) for one in range(pair)], axis=1
    )
    product = lax.dot_general(wide, query_got, NT, preferred_element_type=F32)
    product = product.reshape(owners, pair, docs, total_queries).sum(axis=1)
    extra = jnp.stack([query_high, query_low] + [jnp.zeros_like(query_low)] * 2)
    extra = jnp.broadcast_to(extra[None], (owners,) + extra.shape)
    score_sent = jnp.concatenate([product, extra], axis=1).astype(BF16)
    score_got = lax.all_to_all(score_sent, "fsdp", 0, 0, tiled=True)

    last = jnp.sum(score_got.astype(F32), axis=0)
    doc_row = jnp.pad(doc_sq, (0, total_queries - docs))[None]
    row = jnp.arange(2 * docs)[:, None]
    last = jnp.where(row == docs + 2, doc_row, last)
    last = last + core_swap(last)
    last = last + chip_swap(last, 1)
    last = last + chip_swap(last, 3)
    final = total_queries // group
    factor = 1.0 / math.sqrt(count)
    doc_scale = lax.rsqrt(last[docs + 2, :docs] / count + 1e-06) * factor
    mine = lax.dynamic_slice_in_dim(last[: docs + 2], place * final, final, axis=1)
    query_scale = lax.rsqrt((mine[docs] + mine[docs + 1]) / count + 1e-06)
    return mine[:docs] * doc_scale[:, None] * query_scale[None]


def solution(mesh):
    in_specs = (
        P(None, "fsdp", "tensor"),
        P(None, "fsdp", "tensor"),
        P(None, "fsdp", "tensor"),
        P(None, "fsdp", "tensor"),
        P(None, "tensor"),
        P(None, "tensor"),
        P(),
        P(),
        P("fsdp", None),
        P("fsdp", None, None, "tensor"),
    )
    out_specs = P("fsdp", "tensor")
    return jax.shard_map(body, mesh=mesh, in_specs=in_specs, out_specs=out_specs, check_vma=False)
```

```python
import math

import jax
import jax.numpy as jnp
from jax import lax
from jax.sharding import PartitionSpec as P

F32, BF16 = jnp.float32, jnp.bfloat16
NT = (((1,), (1,)), ((), ()))

MASKS = {"z": 1, "y1": 2, "y3": 6, "x1": 8, "x3": 24}
ORDERS = (
    ("x1", "x3", "y1", "y3"),
    ("x3", "x1", "y3", "y1"),
    ("y1", "y3", "x1", "x3"),
    ("y3", "y1", "x3", "x1"),
)

COMMON = ("x3", "x1", "y3", "y1")


def held_masks(order):
    masks = [0]
    for name in ("z",) + order:
        masks = masks + [mask ^ MASKS[name] for mask in masks]
    return masks


def core_swap(value):
    pairs = [(place, place ^ 1) for place in range(lax.axis_size("tensor"))]
    return lax.ppermute(value, "tensor", pairs)


def chip_shift(value, step):
    size = lax.axis_size("tensor")
    return lax.ppermute(value, "tensor", [(src, (src + 2 * step) % size) for src in range(size)])


def owner_swap(value, step):
    mask = MASKS[step]
    pairs = [(place, place ^ mask) for place in range(lax.axis_size("fsdp"))]
    return lax.ppermute(value, "fsdp", pairs)


def after(value, *others):
    return lax.optimization_barrier((value,) + others)[0]


def tree_gather(block, rider):
    tiles = block.shape[1] // 128
    cuts = [128 * ((tiles * part) // 4) for part in range(5)]
    both = jnp.stack([block, owner_swap(block, "z")])
    chunks = [both[:, :, cuts[part] : cuts[part + 1]] for part in range(4)]
    for step in range(4):
        if step == 3:
            chunks[0], rider = lax.optimization_barrier((chunks[0], rider))
        arrived = [owner_swap(chunk, order[step]) for chunk, order in zip(chunks, ORDERS)]
        chunks = [jnp.concatenate([chunk, new]) for chunk, new in zip(chunks, arrived)]
    return [chunk.reshape(-1, chunk.shape[-1]) for chunk in chunks], cuts, rider


def scale_maps(in_maps, out_maps, col_scale, row_scale):
    scaled = [
        (maps[layer].astype(F32) * scale[layer][None, :]).astype(BF16)
        for maps, scale in ((out_maps, row_scale), (in_maps, col_scale))
        for layer in range(maps.shape[0])
    ]
    return jnp.concatenate(scaled, axis=1)


def common_order(chunk, order):
    parts = chunk.reshape(2, 2, 2, 2, 2, 8, chunk.shape[1])
    axes = [3 - order.index(name) for name in COMMON]
    return parts.transpose(axes + [4, 5, 6]).reshape(chunk.shape)


def one_hot(indices, size):
    return (indices[:, None] == jnp.arange(size, dtype=jnp.int32)[None, :]).astype(F32)


def turned_weights(white_left, white_right, owner, chip, core):
    rows = white_left.shape[1]
    line = jnp.arange(rows, dtype=jnp.int32)
    masks = jnp.asarray(held_masks(COMMON[::-1]), jnp.int32)
    contracted = one_hot((owner ^ jnp.repeat(masks, 8)) * 8 + line % 8, rows)
    away, there = core ^ (line // 128), (chip + line // 32) & 3
    exact = lax.Precision.HIGH
    left_rows = one_hot(128 * away + 32 * there + line % 32, rows)
    right_rows = one_hot(64 * there + 32 * away + line % 32, rows)
    left, right = [], []
    for layer in range(white_left.shape[0]):
        half = jnp.dot(left_rows, white_left[layer], precision=exact)
        left.append(lax.dot_general(half, contracted, NT, precision=exact))
        half = lax.dot_general(
            right_rows, white_right[layer], (((1,), (1,)), ((), ())), precision=exact
        )
        right.append(lax.dot_general(half, contracted, NT, precision=exact))
    return left, right


def absolute_chunks(parts, core, chip):
    two = jnp.roll(parts, 2, axis=2)
    parts = jnp.where(chip >= 2, two, parts)
    one = jnp.roll(parts, 1, axis=2)
    parts = jnp.where(chip % 2 == 1, one, parts)
    return jnp.where(core == 0, parts, parts[:, ::-1])


def tensor_sum(parts):
    jobs, rows, tokens = parts.shape[0], parts.shape[1] // 2, parts.shape[2]
    mine, theirs = parts[:, :rows], parts[:, rows:].astype(BF16)
    other = core_swap(theirs)
    both = (mine + other.astype(F32)).reshape(jobs, 4, rows // 4, tokens)
    sends = [chip_shift(both[:, step].astype(BF16), step) for step in (2, 1, 3)]
    total = both[:, 0] + sends[0].astype(F32) + sends[1].astype(F32) + sends[2].astype(F32)
    return total.astype(BF16)


def chip_swap(value, mask):
    pairs = [(src, src ^ (2 * mask)) for src in range(lax.axis_size("tensor"))]
    return lax.ppermute(value, "tensor", pairs)


def body(
    activations,
    out_grads,
    in_maps,
    out_maps,
    col_scale,
    row_scale,
    white_left,
    white_right,
    doc_lengths,
    queries,
):
    layers, tokens, hidden = activations.shape
    width = out_grads.shape[2]
    owners = lax.axis_size("fsdp")
    group = lax.axis_size("tensor")
    place = lax.axis_index("tensor")
    owner = lax.axis_index("fsdp")
    chip, core = place // 2, place % 2
    docs = doc_lengths.shape[1]
    own_queries, _, kout, kslice = queries.shape
    kin = kslice * group
    total_queries = own_queries * owners
    count = layers * kout * kin
    pair = layers * kslice // owners

    slices = queries.transpose(0, 1, 3, 2).reshape(own_queries, owners, pair * kout)
    slices = slices.transpose(1, 0, 2)
    maps = scale_maps(in_maps, out_maps, col_scale, row_scale)
    chunks, cuts, whites = tree_gather(maps, (white_left, white_right))
    left_weights, right_weights = turned_weights(*whites, owner, chip, core)

    chunks = [common_order(chunk, order) for chunk, order in zip(chunks, ORDERS)]
    parts = []
    for values, low, weights in (
        (out_grads, 0, left_weights),
        (activations, layers * width, right_weights),
    ):
        wide = values.shape[2]
        for layer in range(layers):
            first, total = low + layer * wide, None
            for index in range(4):
                begin, end = max(cuts[index], first), min(cuts[index + 1], first + wide)
                if begin >= end:
                    continue
                block = chunks[index][:, begin - cuts[index] : end - cuts[index]]
                piece = values[layer][:, begin - first : end - first]
                product = lax.dot_general(block, piece, NT, preferred_element_type=F32)
                total = product if total is None else total + product
            parts.append(jnp.dot(weights[layer], total, precision=lax.Precision.HIGH))
    summed = tensor_sum(jnp.stack(parts))
    left, right = summed[:layers], summed[layers:]
    around = [left] + [chip_shift(left, -step) for step in (1, 2, 3)]
    around = jnp.stack(around, axis=1)
    around = jnp.stack([around, core_swap(around)], axis=1)
    left_all = absolute_chunks(around, core, chip).reshape(layers, kout, tokens)

    lengths = doc_lengths[0]
    ends = jnp.cumsum(lengths)
    starts = ends - lengths
    spots = jnp.arange(tokens, dtype=jnp.int32)[None, :]
    member = ((spots >= starts[:, None]) & (spots < ends[:, None])).astype(BF16)
    features = []
    for layer in range(layers):
        masked = (right[layer][:, None, :] * member[None]).reshape(kslice * docs, tokens)
        features.append(
            lax.dot_general(masked, left_all[layer], NT, preferred_element_type=F32)
        )
    features = jnp.stack(features)
    doc_sq = jnp.sum((features * features).reshape(layers * kslice, docs, kout), axis=(0, 2))
    doc_sent = features.astype(BF16).reshape(owners, pair * docs, 2, kout // 2)
    doc_sent = doc_sent.transpose(0, 2, 1, 3).reshape(owners, 2 * pair * docs, kout // 2)
    sent = jnp.concatenate([slices, doc_sent], axis=2)
    got = lax.all_to_all(sent, "fsdp", 0, 0, tiled=True)
    query_got = got[:, :, : pair * kout].reshape(total_queries, pair * kout)
    query_f = query_got.astype(F32)
    query_sq = jnp.sum(query_f * query_f, axis=1)
    query_high = lax.reduce_precision(query_sq, 8, 7)
    query_low = query_sq - query_high

    doc_got = got[:, :, pair * kout :].reshape(owners, 2, pair * docs, kout // 2)
    doc_rows = doc_got.transpose(0, 2, 1, 3).reshape(owners * pair * docs, kout)
    half = (jnp.arange(owners * pair * docs) // docs) % pair
    wide = jnp.concatenate(
        [jnp.where((half == one)[:, None], doc_rows, 0) for one in range(pair)], axis=1
    )
    product = lax.dot_general(wide, query_got, NT, preferred_element_type=F32)
    product = product.reshape(owners, pair, docs, total_queries).sum(axis=1)
    extra = jnp.stack([query_high, query_low] + [jnp.zeros_like(query_low)] * 2)
    extra = jnp.broadcast_to(extra[None], (owners,) + extra.shape)
    score_sent = jnp.concatenate([product, extra], axis=1).astype(BF16)
    score_got = lax.all_to_all(score_sent, "fsdp", 0, 0, tiled=True)

    last = jnp.sum(score_got.astype(F32), axis=0)
    doc_row = jnp.pad(doc_sq, (0, total_queries - docs))[None]
    row = jnp.arange(2 * docs)[:, None]
    last = jnp.where(row == docs + 2, doc_row, last)
    last = last + core_swap(last)
    last = last + chip_swap(last, 1)
    last = last + chip_swap(last, 3)
    final = total_queries // group
    factor = 1.0 / math.sqrt(count)
    doc_scale = lax.rsqrt(last[docs + 2, :docs] / count + 1e-06) * factor
    mine = lax.dynamic_slice_in_dim(last[: docs + 2], place * final, final, axis=1)
    query_scale = lax.rsqrt((mine[docs] + mine[docs + 1]) / count + 1e-06)
    return mine[:docs] * doc_scale[:, None] * query_scale[None]


def solution(mesh):
    in_specs = (
        P(None, "fsdp", "tensor"),
        P(None, "fsdp", "tensor"),
        P(None, "fsdp", "tensor"),
        P(None, "fsdp", "tensor"),
        P(None, "tensor"),
        P(None, "tensor"),
        P(),
        P(),
        P("fsdp", None),
        P("fsdp", None, None, "tensor"),
    )
    out_specs = P("fsdp", "tensor")
    return jax.shard_map(body, mesh=mesh, in_specs=in_specs, out_specs=out_specs, check_vma=False)
```
